32 devices in a mesh: groups: 2 (over x), hidden: 8 (over z, y), seq: 2 (over core).
Axes of the slice: x: 2, y: 2, z: 4, core: 2. Of those that a mesh axis runs over, the one named last changes fastest.
Arguments:
- tokens: bfloat16 [4096, 8192], P(('groups', 'seq'), 'hidden'), parts along dimension 0, may hold values from -6 to 6
- cotangent: bfloat16 [4096, 14336], P(('groups', 'seq'), 'hidden'), parts along dimension 0, may hold values from -6 to 6
- frozen_matrix: bfloat16 [8192, 14336], P('seq', 'hidden'), may hold values from -0.0625 to 0.0625
- adapter_down_factors: bfloat16 [8, 8192, 64], P(None, 'hidden'), may hold values from -0.0625 to 0.0625
- adapter_up_factors: bfloat16 [8, 64, 14336], P(None, None, 'hidden'), may hold values from -0.046875 to 0.046875
- segment_language: int32 [64], P(('groups', 'seq')), parts along dimension 0, may hold values from 0 to 7
- segment_live_rows: int32 [64], P(('groups', 'seq')), parts along dimension 0, may hold values from 1 to 64
- owner: int32 [8], replicated, may hold values from 0 to 7, each once
Outputs:
- input_gradient_features: bfloat16 [8192, 4096], P('hidden', ('groups', 'seq')), parts along dimension 1
- grad_down: float32 [16, 8192, 64], P(('groups', 'hidden')), parts along dimension 0
- grad_up: float32 [16, 64, 14336], P(('groups', 'hidden')), parts along dimension 0
The draws below stay inside these ranges and needn't reach their ends.
There are 2 independent parts, one for each index of `groups`. The reference program is written for one: setup_inputs(seed, part) draws one part's arguments, and reference() takes and returns one part's arrays. A program takes and returns all parts, laid end to end along the dimension named above; an argument that names none is the same for every part. Nothing has to cross between parts.
Inputs may be any that keep to these rules, and one draw needn't show every extreme that they name: owner is a permutation; adapter l is owned by index owner[l] // 1 of hidden.
All inputs are finite; a program needn't handle non-finite values.
Results may differ from the reference program's by a relative error of at most 0.015.
Values may be sent and summed in bfloat16 or wider, within the bound.
A program may use at most 192 MiB of HBM per device.

```python
import math
import jax
import jax.numpy as jnp
import numpy as np
from jax import lax

MODEL_WIDTH = 8192
HIDDEN_HALF = 14336
ADAPTER_RANK = 64
SEG = 64
ADAPTER_COUNT = 8
TOKEN_ROWS = 2048
SEGS = 32
N_HIDDEN = 8


def with_ends(result, own_key, low, high):
    longest = result.shape.index(max(result.shape))
    spots = []
    for shift in (0, 1):
        where = [jax.random.randint(jax.random.fold_in(own_key, axis), (), 0, length) for axis, length in enumerate(result.shape)]
        where[longest] = (where[longest] + shift) % result.shape[longest]
        spots.append(tuple(where))
    return result.at[spots[0]].set(low).at[spots[1]].set(high)


def strengthened(values, key, source, target, parts, factor):
    owner, partner = [(jnp.arange(values.shape[position]) // (values.shape[position] // parts)).reshape([-1 if axis == position else 1 for axis in range(values.ndim)]) for position in (source, target)]
    chosen = jax.random.permutation(key, parts)[partner]
    strong = (owner == chosen) | (owner == (partner + parts // 2) % parts)
    return jnp.where(strong, factor * values, values)


def block_levels(own_key, dims, shards, low, top_value):
    loudness, own = 1.0, jax.random.fold_in(own_key, 6)
    for axis_at, blocks in shards:
        heights = jnp.exp(jax.random.uniform(jax.random.fold_in(own, axis_at), (blocks,), jnp.float32, low / len(shards), top_value / len(shards)))
        loudness = loudness * jnp.repeat(heights, dims[axis_at] // blocks).reshape([-1 if axis == axis_at else 1 for axis in range(len(dims))])
    return loudness


def cumulative_ranks(amount, slope):
    loads = [(1 << 20) // math.isqrt(grade ** slope) + 1 for grade in range(1, amount + 1)]
    scale = 1 + sum(loads) // (1 << 30)
    return np.cumsum(np.array([max(1, weight // scale) for weight in loads]))


def ranked_ids(key, extent, count, skew):
    table = cumulative_ranks(count, skew)
    lot = jax.random.randint(jax.random.fold_in(key, 1), extent, 0, int(table[count - 1]))
    standing = jnp.searchsorted(jnp.asarray(table, jnp.int32), lot, side="right")
    return jax.random.permutation(jax.random.fold_in(key, 2), count)[standing].astype(jnp.int32)


def gaussian(stream_key, extent, scale, limit, shards=(), kind=jnp.bfloat16):
    gain = block_levels(stream_key, extent, shards, -0.22, 0.18) if shards else 1.0
    entries = jax.random.normal(stream_key, extent, jnp.float32) * scale * gain
    return jnp.minimum(jnp.maximum(entries, -limit), limit).astype(kind)


def bell_draw_with(own_key, shape, deviation, limit, pieces, heavy, kind=jnp.bfloat16):
    result = deviation * jax.random.normal(own_key, shape, jnp.float32)
    if pieces:
        result = result * block_levels(own_key, shape, pieces, -0.22, 0.18)
    return jnp.clip(strengthened(result, jax.random.fold_in(own_key, 3), *heavy), -limit, limit).astype(kind)


def setup_inputs(seed: int = 0, part: int = 0) -> dict:
    splits = jax.random.split(jax.random.key(seed), 9)
    own_keys = jax.random.split(jax.random.fold_in(splits[8], part), 9)
    tokens = gaussian(own_keys[0], (TOKEN_ROWS, MODEL_WIDTH), 1.0, 6.0, ((0, 2), (1, 8)))
    cotangent = gaussian(own_keys[1], (TOKEN_ROWS, HIDDEN_HALF), 1.0, 6.0, ((0, 2), (1, 8)))
    frozen_matrix = bell_draw_with(splits[2], (MODEL_WIDTH, HIDDEN_HALF), HIDDEN_HALF ** -0.5, 0.0625, ((0, 2), (1, 8)), (1, 0, 8, 2.0))
    adapter_down_factors = gaussian(splits[3], (ADAPTER_COUNT, MODEL_WIDTH, ADAPTER_RANK), MODEL_WIDTH ** -0.5, 0.0625, ((1, 8),))
    adapter_up_factors = gaussian(splits[4], (ADAPTER_COUNT, ADAPTER_RANK, HIDDEN_HALF), HIDDEN_HALF ** -0.5, 0.046875, ((2, 8),))
    segment_language = with_ends(ranked_ids(own_keys[5], (SEGS,), ADAPTER_COUNT, 2), jax.random.fold_in(own_keys[5], 3), 0, ADAPTER_COUNT - 1).astype(jnp.int32)
    segment_live_rows = with_ends(jax.random.randint(own_keys[6], (SEGS,), 1, SEG + 1), jax.random.fold_in(own_keys[6], 1), 1, SEG).astype(jnp.int32)
    owner = jax.random.permutation(splits[7], ADAPTER_COUNT).astype(jnp.int32)
    return {"tokens": tokens, "cotangent": cotangent, "frozen_matrix": frozen_matrix, "adapter_down_factors": adapter_down_factors, "adapter_up_factors": adapter_up_factors, "segment_language": segment_language, "segment_live_rows": segment_live_rows, "owner": owner}


adapter_scale = 2.0


def reference(tokens, cotangent, frozen_matrix, adapter_down_factors, adapter_up_factors, segment_language, segment_live_rows, owner):
    nseg = TOKEN_ROWS // SEG
    live = (lax.broadcasted_iota(jnp.int32, (nseg, SEG), 1) < segment_live_rows[:, None]).astype(cotangent.dtype)
    masked = (cotangent.reshape(nseg, SEG, HIDDEN_HALF) * live[:, :, None]).astype(jnp.bfloat16)
    rows = tokens.reshape(nseg, SEG, MODEL_WIDTH)
    segment_down_factor = jnp.take(adapter_down_factors, segment_language, axis=0)
    segment_up_factor = jnp.take(adapter_up_factors, segment_language, axis=0)
    low = jnp.einsum('sti,sir->str', rows.astype(jnp.float32), segment_down_factor.astype(jnp.float32)).astype(jnp.bfloat16)
    backward_rows = jnp.einsum('stf,srf->str', masked.astype(jnp.float32), segment_up_factor.astype(jnp.float32)).astype(jnp.bfloat16)
    segment_counts = jax.ops.segment_sum(segment_live_rows.astype(jnp.float32), segment_language, num_segments=ADAPTER_COUNT)
    scale_factor = adapter_scale / jnp.maximum(segment_counts, 1.0)
    da_seg = jnp.einsum('sti,str->sir', rows.astype(jnp.float32), backward_rows.astype(jnp.float32))
    db_seg = jnp.einsum('str,stf->srf', low.astype(jnp.float32), masked.astype(jnp.float32))
    da = jax.ops.segment_sum(da_seg, segment_language, num_segments=ADAPTER_COUNT) * scale_factor[:, None, None]
    db = jax.ops.segment_sum(db_seg, segment_language, num_segments=ADAPTER_COUNT) * scale_factor[:, None, None]
    grad_down = jnp.zeros((ADAPTER_COUNT, MODEL_WIDTH, ADAPTER_RANK), jnp.float32).at[owner].set(da)
    grad_up = jnp.zeros((ADAPTER_COUNT, ADAPTER_RANK, HIDDEN_HALF), jnp.float32).at[owner].set(db)
    flat = masked.reshape(TOKEN_ROWS, HIDDEN_HALF)
    width = HIDDEN_HALF // N_HIDDEN

    def add_block(index, total):
        start = (index * width)
        weight_block = lax.dynamic_slice_in_dim(frozen_matrix, start, width, 1)
        grad_block = lax.dynamic_slice_in_dim(flat, start, width, 1)
        part = jnp.dot(weight_block, grad_block.T, preferred_element_type=jnp.float32)
        return total + part.astype(jnp.bfloat16).astype(jnp.float32)

    frozen_term = lax.fori_loop(0, N_HIDDEN, add_block, jnp.zeros((MODEL_WIDTH, TOKEN_ROWS), jnp.float32))
    adapter_term = jnp.einsum('xuz,xjz->uxj', segment_down_factor.astype(jnp.float32), backward_rows.astype(jnp.float32)).reshape(MODEL_WIDTH, TOKEN_ROWS)
    input_gradient_features = (frozen_term + adapter_scale * adapter_term).astype(jnp.bfloat16)
    return (input_gradient_features, grad_down, grad_up)
```

```python
import jax
import jax.numpy as jnp
from jax import lax
from jax.sharding import PartitionSpec as P

adapter_scale = 2.0
CHUNKS = 2


def dot_rows(left, right):
    return lax.dot_general(
        left, right, (((1,), (1,)), ((), ())), preferred_element_type=jnp.float32
    )


def flows(n_hidden, n_seq):
    depth = n_hidden // 2
    half = depth // n_seq

    def spot(zeta, y, c):
        z = zeta if c == 0 else depth - 1 - zeta
        return (2 * z + y) * n_seq + c

    down, up = [], []
    for r in range(depth - 1):
        down.append(
            [
                (spot(zeta, y, c), spot(zeta - 1, y, c))
                for zeta in range(1, depth)
                if 0 <= r - (depth - 1 - zeta) < min(half, zeta)
                for y in range(2)
                for c in range(n_seq)
            ]
        )
    for q in range(half - 1):
        up.append(
            [
                (spot(zeta, y, c), spot(zeta + 1, y, c))
                for zeta in range(q + 1)
                for y in range(2)
                for c in range(n_seq)
            ]
        )
    return down, up


def pick(blocks, which):
    chosen = blocks[0]
    for index in range(1, len(blocks)):
        chosen = jnp.where(which >= index, blocks[index], chosen)
    return chosen


def local(
    tokens,
    cotangent,
    frozen_matrix,
    adapter_down_factors,
    adapter_up_factors,
    segment_language,
    segment_live_rows,
    owner,
):
    f32, bf16 = jnp.float32, jnp.bfloat16
    nh, ns = lax.axis_size("hidden"), lax.axis_size("seq")
    h, c = lax.axis_index("hidden"), lax.axis_index("seq")
    depth = nh // 2
    half = depth // ns
    y, z = h % 2, h // 2
    zeta = jnp.where(c == 0, z, depth - 1 - z)
    rows, d_local = tokens.shape
    f_local = cotangent.shape[1]
    nseg = segment_language.shape[0]
    seg = rows // nseg
    langs = owner.shape[0]
    rank = adapter_down_factors.shape[2]
    owned = langs // nh
    block = frozen_matrix.shape[0] // (2 * half)
    other = [(i, ns - 1 - i) for i in range(ns)]
    partner = [(i, i ^ 1) for i in range(nh)]
    down_pairs, up_pairs = flows(nh, ns)

    live = (
        lax.broadcasted_iota(jnp.int32, (nseg, seg), 1) < segment_live_rows[:, None]
    ).astype(bf16)
    masked = (cotangent.reshape(nseg, seg, f_local) * live[:, :, None]).reshape(rows, f_local)
    masked_other = lax.ppermute(masked, "seq", other)

    lang_row = jnp.repeat(segment_language, seg)
    slot_row = jnp.repeat(jnp.take(owner, segment_language), seg)
    lang_hot = lang_row[:, None] == jnp.arange(langs, dtype=jnp.int32)[None, :]
    slot_hot = slot_row[:, None] == jnp.arange(langs, dtype=jnp.int32)[None, :]

    def own_language(wide):
        wide = wide.reshape(rows, langs, rank)
        return jnp.sum(jnp.where(lang_hot[:, :, None], wide, 0.0), axis=1)

    def spread(narrow, hot):
        wide = jnp.where(hot[:, :, None], narrow[:, None, :], jnp.zeros((), narrow.dtype))
        return wide.reshape(rows, langs * rank)

    down_cat = adapter_down_factors.transpose(1, 0, 2).reshape(d_local, langs * rank)
    up_cat = adapter_up_factors.reshape(langs * rank, f_local)
    low_part = own_language(jnp.dot(tokens, down_cat, preferred_element_type=f32))
    back_part = own_language(dot_rows(masked, up_cat))
    both = lax.psum(jnp.concatenate([low_part, back_part], axis=1).astype(bf16), "hidden")
    low, back = both[:, :rank], both[:, rank:]
    back_slots = spread(back, slot_hot)
    low_slots = spread(low, slot_hot)
    da = lax.dot_general(
        back_slots, tokens, (((0,), (0,)), ((), ())), preferred_element_type=f32
    ).reshape(langs * rank, ns, d_local // ns)
    db = lax.dot_general(
        low_slots, masked, (((0,), (0,)), ((), ())), preferred_element_type=f32
    ).reshape(langs * rank, ns, f_local // ns)
    terms = jnp.concatenate(
        [
            jnp.concatenate([da[:, i], db[:, i]], axis=1)[None]
            for i in range(ns)
        ],
        axis=0,
    )
    mine = lax.dynamic_index_in_dim(terms, c, 0, keepdims=False)
    theirs = lax.dynamic_index_in_dim(terms, ns - 1 - c, 0, keepdims=False)
    summed = (mine + lax.ppermute(theirs.astype(bf16), "seq", other).astype(f32)).astype(bf16)
    width = summed.shape[1]
    got = lax.all_to_all(
        summed.reshape(nh, owned * rank, width), "hidden", split_axis=0, concat_axis=0, tiled=True
    )
    got_other = lax.ppermute(got, "seq", other)
    first = jnp.where(c == 0, got, got_other)
    last = jnp.where(c == 0, got_other, got)
    slot_seg = jnp.take(owner, segment_language)
    slot_match = slot_seg[None, :] == (h * owned + jnp.arange(owned, dtype=jnp.int32))[:, None]
    count_here = jnp.sum(jnp.where(slot_match, segment_live_rows[None, :], 0), axis=1)
    count = (count_here + lax.ppermute(count_here, "seq", other)).astype(f32)
    factor = (adapter_scale / jnp.maximum(count, 1.0))[:, None, None]
    da_width = d_local // ns

    def assemble(pieces):
        joined = jnp.concatenate(pieces, axis=-1)
        joined = joined.reshape(nh, owned, rank, joined.shape[-1]).transpose(1, 2, 0, 3)
        return joined.reshape(owned, rank, -1).astype(f32) * factor

    grad_down = assemble([first[..., :da_width], last[..., :da_width]]).transpose(0, 2, 1)
    grad_up = assemble([first[..., da_width:], last[..., da_width:]])

    def weight(d, side):
        at = jnp.where(c == 0, d, half - 1 - d)
        return lax.dynamic_slice_in_dim(frozen_matrix, (2 * at + side) * block, block, 0)

    send_weights = [weight(d, 1 - y) for d in range(half)]
    keep_weights = [weight(d, y) for d in range(half)]
    wide = rows // CHUNKS
    results = []
    for source in (masked, masked_other):
        for part in range(CHUNKS):
            piece = source[part * wide : (part + 1) * wide]
            sums = []
            for d in range(half):
                sent = lax.ppermute(
                    dot_rows(send_weights[d], piece).astype(bf16), "hidden", partner
                )
                kept = dot_rows(keep_weights[d], piece).astype(bf16)
                sums.append((kept.astype(f32) + sent.astype(f32)).astype(bf16))
            total = None
            for r, pairs in enumerate(down_pairs):
                value = pick(sums[: r + 1], r - (depth - 1 - zeta))
                if total is not None:
                    value = (value.astype(f32) + total.astype(f32)).astype(bf16)
                total = lax.ppermute(value, ("hidden", "seq"), pairs)
            lifted = None
            for q, pairs in enumerate(up_pairs):
                value = pick(sums, half - 1 - q + zeta)
                if lifted is not None:
                    value = (value.astype(f32) + lifted.astype(f32)).astype(bf16)
                lifted = lax.ppermute(value, ("hidden", "seq"), pairs)
            whole = pick(sums, zeta).astype(f32) + total.astype(f32)
            if lifted is not None:
                whole = whole + lifted.astype(f32)
            results.append(whole)
    owner_core = h // (nh // ns)
    hand_over = [
        (i * ns + i // (nh // ns), i * ns + ns - 1 - i // (nh // ns)) for i in range(nh)
    ]
    base = []
    for part in range(CHUNKS):
        handed = lax.ppermute(
            results[CHUNKS + part].astype(bf16), ("hidden", "seq"), hand_over
        ).astype(f32)
        base.append(jnp.where(c == owner_core, results[part], handed))
    adapter_term = dot_rows(down_cat, spread(back, lang_hot))
    input_gradient_features = (
        jnp.concatenate(base, axis=1) + adapter_scale * adapter_term
    ).astype(bf16)
    return (input_gradient_features, grad_down, grad_up)


def solution(mesh):
    return jax.shard_map(
        local,
        mesh=mesh,
        in_specs=(
            P(("groups", "seq"), "hidden"),
            P(("groups", "seq"), "hidden"),
            P("seq", "hidden"),
            P(None, "hidden", None),
            P(None, None, "hidden"),
            P(("groups", "seq")),
            P(("groups", "seq")),
            P(),
        ),
        out_specs=(
            P("hidden", ("groups", "seq")),
            P(("groups", "hidden"), None, None),
            P(("groups", "hidden"), None, None),
        ),
        check_vma=False,
    )
```

```python
import functools

import jax
import jax.numpy as jnp
from jax import lax
from jax.sharding import PartitionSpec as P

adapter_scale = 2.0
CHUNKS = 2


def dot_rows(left, right):
    return lax.dot_general(
        left, right, (((1,), (1,)), ((), ())), preferred_element_type=jnp.float32
    )


def flows(n_hidden, n_seq):
    depth = n_hidden // 2
    half = depth // n_seq

    def spot(zeta, y, c):
        z = zeta if c == 0 else depth - 1 - zeta
        return (2 * z + y) * n_seq + c

    down, up = [], []
    for r in range(depth - 1):
        down.append(
            [
                (spot(zeta, y, c), spot(zeta - 1, y, c))
                for zeta in range(1, depth)
                if 0 <= r - (depth - 1 - zeta) < min(half, zeta)
                for y in range(2)
                for c in range(n_seq)
            ]
        )
    for q in range(half - 1):
        up.append(
            [
                (spot(zeta, y, c), spot(zeta + 1, y, c))
                for zeta in range(q + 1)
                for y in range(2)
                for c in range(n_seq)
            ]
        )
    return down, up


def pick(blocks, which):
    chosen = blocks[0]
    for index in range(1, len(blocks)):
        chosen = jnp.where(which >= index, blocks[index], chosen)
    return chosen


def local(
    tokens,
    cotangent,
    frozen_matrix,
    adapter_down_factors,
    adapter_up_factors,
    segment_language,
    segment_live_rows,
    owner,
):
    rows = tokens.shape[0]
    live_here = jnp.sum(segment_live_rows).reshape(1)
    shards = lax.axis_size("groups") * lax.axis_size("seq")
    most = live_here
    for step in range(1, shards):
        turn = [(i, (i + step) % shards) for i in range(shards)]
        most = jnp.maximum(most, lax.ppermute(live_here, ("groups", "seq"), turn))
    sizes = [rows * 5 // 8, rows * 3 // 4, rows]
    branch = sum((most[0] > size).astype(jnp.int32) for size in sizes[:-1])
    return lax.switch(
        branch,
        [functools.partial(packed, size) for size in sizes],
        tokens,
        cotangent,
        frozen_matrix,
        adapter_down_factors,
        adapter_up_factors,
        segment_language,
        segment_live_rows,
        owner,
    )


def packed(
    size,
    tokens,
    cotangent,
    frozen_matrix,
    adapter_down_factors,
    adapter_up_factors,
    segment_language,
    segment_live_rows,
    owner,
):
    f32, bf16 = jnp.float32, jnp.bfloat16
    nh, ns = lax.axis_size("hidden"), lax.axis_size("seq")
    h, c = lax.axis_index("hidden"), lax.axis_index("seq")
    depth = nh // 2
    half = depth // ns
    y, z = h % 2, h // 2
    zeta = jnp.where(c == 0, z, depth - 1 - z)
    rows, d_local = tokens.shape
    f_local = cotangent.shape[1]
    nseg = segment_language.shape[0]
    seg = rows // nseg
    langs = owner.shape[0]
    rank = adapter_down_factors.shape[2]
    owned = langs // nh
    block = frozen_matrix.shape[0] // (2 * half)
    other = [(i, ns - 1 - i) for i in range(ns)]
    partner = [(i, i ^ 1) for i in range(nh)]
    down_pairs, up_pairs = flows(nh, ns)

    order = jnp.arange(nseg, dtype=jnp.int32)
    begins = jnp.sum(jnp.where(order[None, :] < order[:, None], segment_live_rows[None, :], 0), 1)
    step = lax.broadcasted_iota(jnp.int32, (nseg, seg), 1)
    place = jnp.where(step < segment_live_rows[:, None], begins[:, None] + step, -1)
    slots = jnp.arange(size, dtype=jnp.int32)
    pack = (slots[:, None] == place.reshape(1, rows)).astype(bf16)
    masked = jnp.dot(pack, cotangent, preferred_element_type=f32).astype(bf16)
    masked_other = lax.ppermute(masked, "seq", other)

    def weight(d, side):
        at = jnp.where(c == 0, d, half - 1 - d)
        return lax.dynamic_slice_in_dim(frozen_matrix, (2 * at + side) * block, block, 0)

    send_weights = [weight(d, 1 - y) for d in range(half)]
    keep_weights = [weight(d, y) for d in range(half)]
    wide = size // CHUNKS
    pieces = [
        source[part * wide : (part + 1) * wide]
        for source in (masked, masked_other)
        for part in range(CHUNKS)
    ]
    outgoing = [
        [dot_rows(piece, send_weights[d]).astype(bf16) for d in range(half)] for piece in pieces
    ]
    incoming = [[lax.ppermute(part, "hidden", partner) for part in parts] for parts in outgoing]

    rows_packed = jnp.dot(pack, tokens, preferred_element_type=f32).astype(bf16)
    inside = (slots[:, None] >= begins[None, :]) & (
        slots[:, None] < (begins + segment_live_rows)[None, :]
    )
    slot_seg = jnp.take(owner, segment_language)
    lang_row = jnp.sum(jnp.where(inside, segment_language[None, :] + 1, 0), axis=1) - 1
    slot_row = jnp.sum(jnp.where(inside, slot_seg[None, :] + 1, 0), axis=1) - 1
    lang_hot = lang_row[:, None] == jnp.arange(langs, dtype=jnp.int32)[None, :]
    slot_hot = slot_row[:, None] == jnp.arange(langs, dtype=jnp.int32)[None, :]

    def own_language(every):
        every = every.reshape(size, langs, rank)
        return jnp.sum(jnp.where(lang_hot[:, :, None], every, 0.0), axis=1)

    def spread(narrow, hot):
        every = jnp.where(hot[:, :, None], narrow[:, None, :], jnp.zeros((), narrow.dtype))
        return every.reshape(size, langs * rank)

    down_cat = adapter_down_factors.transpose(1, 0, 2).reshape(d_local, langs * rank)
    up_cat = adapter_up_factors.reshape(langs * rank, f_local)
    low_part = own_language(jnp.dot(rows_packed, down_cat, preferred_element_type=f32))
    back_part = own_language(dot_rows(masked, up_cat))
    both = lax.psum(jnp.concatenate([low_part, back_part], axis=1).astype(bf16), "hidden")

    kept = [
        [dot_rows(piece, keep_weights[d]).astype(bf16) for d in range(half)] for piece in pieces
    ]
    first_in, outgoing, kept = lax.optimization_barrier((incoming[0], outgoing, kept))
    incoming[0] = first_in
    both, halfway = lax.optimization_barrier((both, incoming[CHUNKS - 1]))
    incoming[CHUNKS - 1] = halfway

    low, back = both[:, :rank], both[:, rank:]
    back_slots = spread(back, slot_hot)
    low_slots = spread(low, slot_hot)
    da = lax.dot_general(
        back_slots, rows_packed, (((0,), (0,)), ((), ())), preferred_element_type=f32
    ).reshape(langs * rank, ns, d_local // ns)
    db = lax.dot_general(
        low_slots, masked, (((0,), (0,)), ((), ())), preferred_element_type=f32
    ).reshape(langs * rank, ns, f_local // ns)
    terms = jnp.stack([jnp.concatenate([da[:, i], db[:, i]], axis=1) for i in range(ns)])
    mine = lax.dynamic_index_in_dim(terms, c, 0, keepdims=False)
    theirs = lax.dynamic_index_in_dim(terms, ns - 1 - c, 0, keepdims=False)
    summed = (mine + lax.ppermute(theirs.astype(bf16), "seq", other).astype(f32)).astype(bf16)
    width = summed.shape[1]
    got = lax.all_to_all(
        summed.reshape(nh, owned * rank, width), "hidden", split_axis=0, concat_axis=0, tiled=True
    )
    got_other = lax.ppermute(got, "seq", other)
    first = jnp.where(c == 0, got, got_other)
    last = jnp.where(c == 0, got_other, got)
    slot_match = slot_seg[None, :] == (h * owned + jnp.arange(owned, dtype=jnp.int32))[:, None]
    count_here = jnp.sum(jnp.where(slot_match, segment_live_rows[None, :], 0), axis=1)
    count = (count_here + lax.ppermute(count_here, "seq", other)).astype(f32)
    factor = (adapter_scale / jnp.maximum(count, 1.0))[:, None, None]
    da_width = d_local // ns

    def assemble(halves):
        joined = jnp.concatenate(halves, axis=-1)
        joined = joined.reshape(nh, owned, rank, joined.shape[-1]).transpose(1, 2, 0, 3)
        return joined.reshape(owned, rank, -1).astype(f32) * factor

    grad_down = assemble([first[..., :da_width], last[..., :da_width]]).transpose(0, 2, 1)
    grad_up = assemble([first[..., da_width:], last[..., da_width:]])

    results = []
    for mine_parts, their_parts in zip(kept, incoming):
        sums = [
            (own.astype(f32) + came.astype(f32)).astype(bf16)
            for own, came in zip(mine_parts, their_parts)
        ]
        total = None
        for r, pairs in enumerate(down_pairs):
            value = pick(sums[: r + 1], r - (depth - 1 - zeta))
            if total is not None:
                value = (value.astype(f32) + total.astype(f32)).astype(bf16)
            total = lax.ppermute(value, ("hidden", "seq"), pairs)
        lifted = None
        for q, pairs in enumerate(up_pairs):
            value = pick(sums, half - 1 - q + zeta)
            if lifted is not None:
                value = (value.astype(f32) + lifted.astype(f32)).astype(bf16)
            lifted = lax.ppermute(value, ("hidden", "seq"), pairs)
        whole = pick(sums, zeta).astype(f32) + total.astype(f32)
        if lifted is not None:
            whole = whole + lifted.astype(f32)
        results.append(whole)
    owner_core = h // (nh // ns)
    hand_over = [
        (i * ns + i // (nh // ns), i * ns + ns - 1 - i // (nh // ns)) for i in range(nh)
    ]
    adapter_term = dot_rows(spread(back, lang_hot), down_cat)
    gradient = []
    for part in range(CHUNKS):
        handed = lax.ppermute(
            results[CHUNKS + part].astype(bf16), ("hidden", "seq"), hand_over
        ).astype(f32)
        base = jnp.where(c == owner_core, results[part], handed)
        low_rank = adapter_term[part * wide : (part + 1) * wide]
        gradient.append((base + adapter_scale * low_rank).astype(bf16))
    input_gradient_features = lax.dot_general(
        jnp.concatenate(gradient, axis=0),
        pack,
        (((0,), (0,)), ((), ())),
        preferred_element_type=f32,
    ).astype(bf16)
    return (input_gradient_features, grad_down, grad_up)


def solution(mesh):
    return jax.shard_map(
        local,
        mesh=mesh,
        in_specs=(
            P(("groups", "seq"), "hidden"),
            P(("groups", "seq"), "hidden"),
            P("seq", "hidden"),
            P(None, "hidden", None),
            P(None, None, "hidden"),
            P(("groups", "seq")),
            P(("groups", "seq")),
            P(),
        ),
        out_specs=(
            P("hidden", ("groups", "seq")),
            P(("groups", "hidden"), None, None),
            P(("groups", "hidden"), None, None),
        ),
        check_vma=False,
    )
```

```python
import functools

import jax
import jax.numpy as jnp
from jax import lax
from jax.sharding import PartitionSpec as P

adapter_scale = 2.0
CHUNKS = 2


def dot_rows(left, right):
    return lax.dot_general(
        left, right, (((1,), (1,)), ((), ())), preferred_element_type=jnp.float32
    )


def flows(n_hidden, n_seq):
    depth = n_hidden // 2
    half = depth // n_seq

    def spot(zeta, y, c):
        z = zeta if c == 0 else depth - 1 - zeta
        return (2 * z + y) * n_seq + c

    rounds = []
    for r in range(depth - 1):
        falls = [
            (zeta, zeta - 1)
            for zeta in range(1, depth)
            if 0 <= r - (depth - 1 - zeta) < min(half, zeta)
        ]
        lifts = [(zeta, zeta + 1) for zeta in range(r + 1)] if r < half - 1 else []
        rounds.append(
            [
                (spot(source, y, c), spot(target, y, c))
                for source, target in falls + lifts
                for y in range(2)
                for c in range(n_seq)
            ]
        )
    return rounds


def pick(blocks, which):
    chosen = blocks[0]
    for index in range(1, len(blocks)):
        chosen = jnp.where(which >= index, blocks[index], chosen)
    return chosen


def local(
    tokens,
    cotangent,
    frozen_matrix,
    adapter_down_factors,
    adapter_up_factors,
    segment_language,
    segment_live_rows,
    owner,
):
    rows = tokens.shape[0]
    live_here = jnp.sum(segment_live_rows).reshape(1)
    shards = lax.axis_size("groups") * lax.axis_size("seq")
    most = live_here
    for step in range(1, shards):
        turn = [(i, (i + step) % shards) for i in range(shards)]
        most = jnp.maximum(most, lax.ppermute(live_here, ("groups", "seq"), turn))
    sizes = [rows * 5 // 8, rows * 3 // 4, rows]
    branch = sum((most[0] > size).astype(jnp.int32) for size in sizes[:-1])
    return lax.switch(
        branch,
        [functools.partial(packed, size) for size in sizes],
        tokens,
        cotangent,
        frozen_matrix,
        adapter_down_factors,
        adapter_up_factors,
        segment_language,
        segment_live_rows,
        owner,
    )


def packed(
    size,
    tokens,
    cotangent,
    frozen_matrix,
    adapter_down_factors,
    adapter_up_factors,
    segment_language,
    segment_live_rows,
    owner,
):
    f32, bf16 = jnp.float32, jnp.bfloat16
    nh, ns = lax.axis_size("hidden"), lax.axis_size("seq")
    h, c = lax.axis_index("hidden"), lax.axis_index("seq")
    depth = nh // 2
    half = depth // ns
    y, z = h % 2, h // 2
    zeta = jnp.where(c == 0, z, depth - 1 - z)
    rows, d_local = tokens.shape
    f_local = cotangent.shape[1]
    nseg = segment_language.shape[0]
    seg = rows // nseg
    langs = owner.shape[0]
    rank = adapter_down_factors.shape[2]
    owned = langs // nh
    block = frozen_matrix.shape[0] // (2 * half)
    other = [(i, ns - 1 - i) for i in range(ns)]
    partner = [(i, i ^ 1) for i in range(nh)]
    chain_pairs = flows(nh, ns)

    order = jnp.arange(nseg, dtype=jnp.int32)
    begins = jnp.sum(jnp.where(order[None, :] < order[:, None], segment_live_rows[None, :], 0), 1)
    step = lax.broadcasted_iota(jnp.int32, (nseg, seg), 1)
    place = jnp.where(step < segment_live_rows[:, None], begins[:, None] + step, -1)
    slots = jnp.arange(size, dtype=jnp.int32)
    pack = (slots[:, None] == place.reshape(1, rows)).astype(bf16)
    masked = jnp.dot(pack, cotangent, preferred_element_type=f32).astype(bf16)
    masked_other = lax.ppermute(masked, "seq", other)

    weights = frozen_matrix.reshape(half, 2, block, f_local)

    def side_of(side):
        return lax.dynamic_index_in_dim(weights, side, 1, keepdims=False).reshape(
            half * block, f_local
        )

    send_weights = side_of(1 - y)
    keep_weights = side_of(y)
    wide = size // CHUNKS
    pieces = [
        source[part * wide : (part + 1) * wide]
        for source in (masked, masked_other)
        for part in range(CHUNKS)
    ]
    outgoing = [dot_rows(piece, send_weights).astype(bf16) for piece in pieces]
    incoming = [lax.ppermute(part, "hidden", partner) for part in outgoing]

    rows_packed = jnp.dot(pack, tokens, preferred_element_type=f32).astype(bf16)
    inside = (slots[:, None] >= begins[None, :]) & (
        slots[:, None] < (begins + segment_live_rows)[None, :]
    )
    slot_seg = jnp.take(owner, segment_language)
    lang_row = jnp.sum(jnp.where(inside, segment_language[None, :] + 1, 0), axis=1) - 1
    slot_row = jnp.sum(jnp.where(inside, slot_seg[None, :] + 1, 0), axis=1) - 1
    lang_hot = lang_row[:, None] == jnp.arange(langs, dtype=jnp.int32)[None, :]
    slot_hot = slot_row[:, None] == jnp.arange(langs, dtype=jnp.int32)[None, :]

    def own_language(every):
        every = every.reshape(size, langs, rank)
        return jnp.sum(jnp.where(lang_hot[:, :, None], every, 0.0), axis=1)

    def spread(narrow, hot):
        every = jnp.where(hot[:, :, None], narrow[:, None, :], jnp.zeros((), narrow.dtype))
        return every.reshape(size, langs * rank)

    down_cat = adapter_down_factors.transpose(1, 0, 2).reshape(d_local, langs * rank)
    up_cat = adapter_up_factors.reshape(langs * rank, f_local)
    low_part = own_language(jnp.dot(rows_packed, down_cat, preferred_element_type=f32))
    back_part = own_language(dot_rows(masked, up_cat))
    both = lax.psum(jnp.concatenate([low_part, back_part], axis=1).astype(bf16), "hidden")

    kept = [dot_rows(piece, keep_weights).astype(bf16) for piece in pieces]
    both = both + incoming[CHUNKS - 1][:1, :1] * jnp.zeros((), bf16)
    sent = sum(part[:1, :1] for part in outgoing[CHUNKS:])
    kept[0] = kept[0] + sent * jnp.zeros((), bf16)

    low, back = both[:, :rank], both[:, rank:]
    back_slots = spread(back, slot_hot)
    low_slots = spread(low, slot_hot)
    da = lax.dot_general(
        back_slots, rows_packed, (((0,), (0,)), ((), ())), preferred_element_type=f32
    ).reshape(langs * rank, ns, d_local // ns)
    db = lax.dot_general(
        low_slots, masked, (((0,), (0,)), ((), ())), preferred_element_type=f32
    ).reshape(langs * rank, ns, f_local // ns)
    terms = jnp.stack([jnp.concatenate([da[:, i], db[:, i]], axis=1) for i in range(ns)])
    mine = lax.dynamic_index_in_dim(terms, c, 0, keepdims=False)
    theirs = lax.dynamic_index_in_dim(terms, ns - 1 - c, 0, keepdims=False)
    summed = (mine + lax.ppermute(theirs.astype(bf16), "seq", other).astype(f32)).astype(bf16)
    width = summed.shape[1]
    got = lax.all_to_all(
        summed.reshape(nh, owned * rank, width), "hidden", split_axis=0, concat_axis=0, tiled=True
    )
    got_other = lax.ppermute(got, "seq", other)
    first = jnp.where(c == 0, got, got_other)
    last = jnp.where(c == 0, got_other, got)
    slot_match = slot_seg[None, :] == (h * owned + jnp.arange(owned, dtype=jnp.int32))[:, None]
    count_here = jnp.sum(jnp.where(slot_match, segment_live_rows[None, :], 0), axis=1)
    count = (count_here + lax.ppermute(count_here, "seq", other)).astype(f32)
    factor = (adapter_scale / jnp.maximum(count, 1.0))[:, None, None]
    da_width = d_local // ns

    def assemble(halves):
        joined = jnp.concatenate(halves, axis=-1)
        joined = joined.reshape(nh, owned, rank, joined.shape[-1]).transpose(1, 2, 0, 3)
        return joined.reshape(owned, rank, -1).astype(f32) * factor

    grad_down = assemble([first[..., :da_width], last[..., :da_width]]).transpose(0, 2, 1)
    grad_up = assemble([first[..., da_width:], last[..., da_width:]])

    results = []
    for mine_part, their_part in zip(kept, incoming):
        added = (mine_part.astype(f32) + their_part.astype(f32)).astype(bf16)
        sums = [added[:, d * block : (d + 1) * block] for d in range(half)]

        def block_for(d):
            return pick(sums, jnp.where(c == 0, d, half - 1 - d))

        came, lifted = None, None
        for r, pairs in enumerate(chain_pairs):
            falling = r - (depth - 1 - zeta)
            value = block_for(jnp.where(falling >= 0, falling, half - 1 - r + zeta))
            if came is not None:
                value = (value.astype(f32) + came.astype(f32)).astype(bf16)
            came = lax.ppermute(value, ("hidden", "seq"), pairs)
            if r == half - 2:
                lifted = came
        whole = block_for(zeta).astype(f32) + came.astype(f32)
        if lifted is not None:
            whole = whole + lifted.astype(f32)
        results.append(whole)
    owner_core = h // (nh // ns)
    hand_over = [
        (i * ns + i // (nh // ns), i * ns + ns - 1 - i // (nh // ns)) for i in range(nh)
    ]
    adapter_term = dot_rows(spread(back, lang_hot), down_cat)
    gradient = []
    for part in range(CHUNKS):
        handed = lax.ppermute(
            results[CHUNKS + part].astype(bf16), ("hidden", "seq"), hand_over
        ).astype(f32)
        base = jnp.where(c == owner_core, results[part], handed)
        low_rank = adapter_term[part * wide : (part + 1) * wide]
        gradient.append((base + adapter_scale * low_rank).astype(bf16))
    input_gradient_features = lax.dot_general(
        jnp.concatenate(gradient, axis=0),
        pack,
        (((0,), (0,)), ((), ())),
        preferred_element_type=f32,
    ).astype(bf16)
    return (input_gradient_features, grad_down, grad_up)


def solution(mesh):
    return jax.shard_map(
        local,
        mesh=mesh,
        in_specs=(
            P(("groups", "seq"), "hidden"),
            P(("groups", "seq"), "hidden"),
            P("seq", "hidden"),
            P(None, "hidden", None),
            P(None, None, "hidden"),
            P(("groups", "seq")),
            P(("groups", "seq")),
            P(),
        ),
        out_specs=(
            P("hidden", ("groups", "seq")),
            P(("groups", "hidden"), None, None),
            P(("groups", "hidden"), None, None),
        ),
        check_vma=False,
    )
```

```python
import functools

import jax
import jax.numpy as jnp
from jax import lax
from jax.sharding import PartitionSpec as P

adapter_scale = 2.0
CHUNKS = 2


def dot_rows(left, right):
    return lax.dot_general(
        left, right, (((1,), (1,)), ((), ())), preferred_element_type=jnp.float32
    )


def flows(n_hidden, n_seq):
    depth = n_hidden // 2
    half = depth // n_seq

    def spot(zeta, y, c):
        z = zeta if c == 0 else depth - 1 - zeta
        return (2 * z + y) * n_seq + c

    rounds = []
    for r in range(depth - 1):
        falls = [
            (zeta, zeta - 1)
            for zeta in range(1, depth)
            if 0 <= r - (depth - 1 - zeta) < min(half, zeta)
        ]
        lifts = [(zeta, zeta + 1) for zeta in range(r + 1)] if r < half - 1 else []
        rounds.append(
            [
                (spot(source, y, c), spot(target, y, c))
                for source, target in falls + lifts
                for y in range(2)
                for c in range(n_seq)
            ]
        )
    return rounds


def pick(blocks, which):
    chosen = blocks[0]
    for index in range(1, len(blocks)):
        chosen = jnp.where(which >= index, blocks[index], chosen)
    return chosen


def local(
    tokens,
    cotangent,
    frozen_matrix,
    adapter_down_factors,
    adapter_up_factors,
    segment_language,
    segment_live_rows,
    owner,
):
    rows = tokens.shape[0]
    live_here = jnp.sum(segment_live_rows).reshape(1)
    shards = lax.axis_size("groups") * lax.axis_size("seq")
    most = live_here
    for step in range(1, shards):
        turn = [(i, (i + step) % shards) for i in range(shards)]
        most = jnp.maximum(most, lax.ppermute(live_here, ("groups", "seq"), turn))
    sizes = [rows * 5 // 8, rows * 3 // 4, rows]
    branch = sum((most[0] > size).astype(jnp.int32) for size in sizes[:-1])
    return lax.switch(
        branch,
        [functools.partial(packed, size) for size in sizes],
        tokens,
        cotangent,
        frozen_matrix,
        adapter_down_factors,
        adapter_up_factors,
        segment_language,
        segment_live_rows,
        owner,
    )


def packed(
    size,
    tokens,
    cotangent,
    frozen_matrix,
    adapter_down_factors,
    adapter_up_factors,
    segment_language,
    segment_live_rows,
    owner,
):
    f32, bf16 = jnp.float32, jnp.bfloat16
    nh, ns = lax.axis_size("hidden"), lax.axis_size("seq")
    h, c = lax.axis_index("hidden"), lax.axis_index("seq")
    depth = nh // 2
    half = depth // ns
    y, z = h % 2, h // 2
    zeta = jnp.where(c == 0, z, depth - 1 - z)
    rows, d_local = tokens.shape
    f_local = cotangent.shape[1]
    nseg = segment_language.shape[0]
    seg = rows // nseg
    langs = owner.shape[0]
    rank = adapter_down_factors.shape[2]
    owned = langs // nh
    block = frozen_matrix.shape[0] // (2 * half)
    other = [(i, ns - 1 - i) for i in range(ns)]
    partner = [(i, i ^ 1) for i in range(nh)]
    chain_pairs = flows(nh, ns)

    order = jnp.arange(nseg, dtype=jnp.int32)
    begins = jnp.sum(jnp.where(order[None, :] < order[:, None], segment_live_rows[None, :], 0), 1)
    step = lax.broadcasted_iota(jnp.int32, (nseg, seg), 1)
    place = jnp.where(step < segment_live_rows[:, None], begins[:, None] + step, -1)
    slots = jnp.arange(size, dtype=jnp.int32)
    pack = (slots[:, None] == place.reshape(1, rows)).astype(bf16)
    masked = jnp.dot(pack, cotangent, preferred_element_type=f32).astype(bf16)
    masked_other = lax.ppermute(masked, "seq", other)

    weights = frozen_matrix.reshape(half, 2, block, f_local)

    def side_of(side):
        return lax.dynamic_index_in_dim(weights, side, 1, keepdims=False).reshape(
            half * block, f_local
        )

    send_weights = side_of(1 - y)
    keep_weights = side_of(y)
    wide = size // CHUNKS
    pieces = [
        source[part * wide : (part + 1) * wide]
        for source in (masked, masked_other)
        for part in range(CHUNKS)
    ]
    outgoing = [dot_rows(piece, send_weights).astype(bf16) for piece in pieces]
    incoming = [lax.ppermute(part, "hidden", partner) for part in outgoing]

    rows_packed = jnp.dot(pack, tokens, preferred_element_type=f32).astype(bf16)
    inside = (slots[:, None] >= begins[None, :]) & (
        slots[:, None] < (begins + segment_live_rows)[None, :]
    )
    slot_seg = jnp.take(owner, segment_language)
    lang_row = jnp.sum(jnp.where(inside, segment_language[None, :] + 1, 0), axis=1) - 1
    slot_row = jnp.sum(jnp.where(inside, slot_seg[None, :] + 1, 0), axis=1) - 1
    lang_hot = lang_row[:, None] == jnp.arange(langs, dtype=jnp.int32)[None, :]
    slot_hot = slot_row[:, None] == jnp.arange(langs, dtype=jnp.int32)[None, :]

    def own_language(every):
        every = every.reshape(size, langs, rank)
        return jnp.sum(jnp.where(lang_hot[:, :, None], every, 0.0), axis=1)

    def spread(narrow, hot):
        every = jnp.where(hot[:, :, None], narrow[:, None, :], jnp.zeros((), narrow.dtype))
        return every.reshape(size, langs * rank)

    down_cat = adapter_down_factors.transpose(1, 0, 2).reshape(d_local, langs * rank)
    up_cat = adapter_up_factors.reshape(langs * rank, f_local)
    low_part = own_language(jnp.dot(rows_packed, down_cat, preferred_element_type=f32))
    back_part = own_language(dot_rows(masked, up_cat))
    both = lax.psum(jnp.concatenate([low_part, back_part], axis=1).astype(bf16), "hidden")

    kept = [dot_rows(piece, keep_weights).astype(bf16) for piece in pieces]
    sent = sum(part[:1, :1] for part in outgoing[CHUNKS:])
    kept[0] = kept[0] + sent * jnp.zeros((), bf16)
    both = both + (incoming[CHUNKS][:1, :1] + sent) * jnp.zeros((), bf16)

    low, back = both[:, :rank], both[:, rank:]
    back_slots = spread(back, slot_hot)
    low_slots = spread(low, slot_hot)
    da = lax.dot_general(
        back_slots, rows_packed, (((0,), (0,)), ((), ())), preferred_element_type=f32
    ).reshape(langs * rank, ns, d_local // ns)
    db = lax.dot_general(
        low_slots, masked, (((0,), (0,)), ((), ())), preferred_element_type=f32
    ).reshape(langs * rank, ns, f_local // ns)
    terms = jnp.stack([jnp.concatenate([da[:, i], db[:, i]], axis=1) for i in range(ns)])
    mine = lax.dynamic_index_in_dim(terms, c, 0, keepdims=False)
    theirs = lax.dynamic_index_in_dim(terms, ns - 1 - c, 0, keepdims=False)
    summed = (mine + lax.ppermute(theirs.astype(bf16), "seq", other).astype(f32)).astype(bf16)
    width = summed.shape[1]
    got = lax.all_to_all(
        summed.reshape(nh, owned * rank, width), "hidden", split_axis=0, concat_axis=0, tiled=True
    )
    got_other = lax.ppermute(got, "seq", other)
    first = jnp.where(c == 0, got, got_other)
    last = jnp.where(c == 0, got_other, got)
    slot_match = slot_seg[None, :] == (h * owned + jnp.arange(owned, dtype=jnp.int32))[:, None]
    count_here = jnp.sum(jnp.where(slot_match, segment_live_rows[None, :], 0), axis=1)
    count = (count_here + lax.ppermute(count_here, "seq", other)).astype(f32)
    factor = (adapter_scale / jnp.maximum(count, 1.0))[:, None, None]
    da_width = d_local // ns

    def assemble(halves):
        joined = jnp.concatenate(halves, axis=-1)
        joined = joined.reshape(nh, owned, rank, joined.shape[-1]).transpose(1, 2, 0, 3)
        return joined.reshape(owned, rank, -1).astype(f32) * factor

    grad_down = assemble([first[..., :da_width], last[..., :da_width]]).transpose(0, 2, 1)
    grad_up = assemble([first[..., da_width:], last[..., da_width:]])

    results = []
    for mine_part, their_part in zip(kept, incoming):
        added = (mine_part.astype(f32) + their_part.astype(f32)).astype(bf16)
        sums = [added[:, d * block : (d + 1) * block] for d in range(half)]

        def block_for(d):
            return pick(sums, jnp.where(c == 0, d, half - 1 - d))

        came, lifted = None, None
        for r, pairs in enumerate(chain_pairs):
            falling = r - (depth - 1 - zeta)
            value = block_for(jnp.where(falling >= 0, falling, half - 1 - r + zeta))
            if came is not None:
                value = (value.astype(f32) + came.astype(f32)).astype(bf16)
            came = lax.ppermute(value, ("hidden", "seq"), pairs)
            if r == half - 2:
                lifted = came
        whole = block_for(zeta).astype(f32) + came.astype(f32)
        if lifted is not None:
            whole = whole + lifted.astype(f32)
        results.append(whole)
    owner_core = h // (nh // ns)
    hand_over = [
        (i * ns + i // (nh // ns), i * ns + ns - 1 - i // (nh // ns)) for i in range(nh)
    ]
    adapter_term = dot_rows(spread(back, lang_hot), down_cat)
    gradient = []
    for part in range(CHUNKS):
        handed = lax.ppermute(
            results[CHUNKS + part].astype(bf16), ("hidden", "seq"), hand_over
        ).astype(f32)
        base = jnp.where(c == owner_core, results[part], handed)
        low_rank = adapter_term[part * wide : (part + 1) * wide]
        gradient.append((base + adapter_scale * low_rank).astype(bf16))
    input_gradient_features = lax.dot_general(
        jnp.concatenate(gradient, axis=0),
        pack,
        (((0,), (0,)), ((), ())),
        preferred_element_type=f32,
    ).astype(bf16)
    return (input_gradient_features, grad_down, grad_up)


def solution(mesh):
    return jax.shard_map(
        local,
        mesh=mesh,
        in_specs=(
            P(("groups", "seq"), "hidden"),
            P(("groups", "seq"), "hidden"),
            P("seq", "hidden"),
            P(None, "hidden", None),
            P(None, None, "hidden"),
            P(("groups", "seq")),
            P(("groups", "seq")),
            P(),
        ),
        out_specs=(
            P("hidden", ("groups", "seq")),
            P(("groups", "hidden"), None, None),
            P(("groups", "hidden"), None, None),
        ),
        check_vma=False,
    )
```
